256 devices in a mesh: gx: 4 (over x), gy: 8 (over z), gz: 8 (over y, core).
Axes of the slice: x: 4, y: 4, z: 8, core: 2. Of those that a mesh axis runs over, the one named last changes fastest.
Arguments:
- residual: bfloat16 [4, 8, 8, 512, 1536], P('gx', 'gy', 'gz'), may hold values from -6 to 6
- schur_inverse: bfloat16 [4, 8, 8, 1536, 1536], P('gx', 'gy', 'gz'), may hold values from -0.15625 to 0.15625
- coarse_basis: bfloat16 [4, 8, 8, 128, 1536], P('gx', 'gy', 'gz'), may hold values from -0.25 to 0.25
- coarse_index: int32 [4, 8, 8, 128], P('gx', 'gy', 'gz'), may hold values from 0 to 511
- block_slot: int32 [4, 8, 8, 12], P('gx', 'gy', 'gz'), may hold values from 0 to 1, as said below
- group_inverse: float32 [4, 8, 512, 512], P('gx', 'gy'), may hold values from -0.25 to 0.25
- group_restrict: float32 [4, 8, 512, 512], P('gx', 'gy'), may hold values from -0.25 to 0.25
- top_inverse: float32 [512, 512], replicated, may hold values from -0.046875 to 0.046875
Outputs:
- correction: bfloat16 [4, 8, 8, 512, 1536], P('gx', 'gy', 'gz')
The draws below stay inside these ranges and needn't reach their ends.
Inputs may be any that keep to these rules, and one draw needn't show every extreme that they name: `block_slot`: for every subdomain and face, the 2 entries of that face are a permutation of 0 to 1.
All inputs are finite; a program needn't handle non-finite values.
Results may differ from the reference program's by a relative error of at most 0.0055.
Values may be sent and summed in bfloat16 or wider, within the bound.
No kernel may reach another device: no remote copies, remote signals or barrier semaphores. Data moves between devices by JAX's collectives and lax.ppermute only.
A program may use at most 64 MiB of HBM per device.

```python
import jax
import jax.numpy as jnp
from jax import lax

BW = 128
FB = 2
NC = 128
C2 = 512
C3 = 512
R = 512
NI = 1536
SX = 4
SY = 8
SZ = 8


def draw_block_slot(key, part):
    key = jax.random.fold_in(key, 7)
    total_faces = SX * SY * SZ * 6
    keys = jax.random.split(key, total_faces)
    orders = jax.vmap(lambda k: jax.random.permutation(k, FB))(keys)
    return orders.reshape(SX, SY, SZ, 6 * FB).astype(jnp.int32)


def plant(entries, key, low, top_value):
    place = [jax.random.randint(jax.random.fold_in(key, axis), (), 0, length) for axis, length in enumerate(entries.shape)]
    widest = entries.shape.index(max(entries.shape))
    beside = place[:widest] + [(place[widest] + 1) % entries.shape[widest]] + place[widest + 1:]
    return entries.at[tuple(place)].set(low).at[tuple(beside)].set(top_value)


def block_levels(stream_key, dims, shards, smallest, high):
    factor_of, own = 1.0, jax.random.fold_in(stream_key, 6)
    for dim, blocks in shards:
        steps = jnp.exp(jax.random.uniform(jax.random.fold_in(own, dim), (blocks,), jnp.float32, smallest / len(shards), high / len(shards)))
        factor_of = factor_of * jnp.repeat(steps, dims[dim] // blocks).reshape([-1 if axis == dim else 1 for axis in range(len(dims))])
    return factor_of


def bell_draw(rng, shape, width, limit, cuts=(), dtype=jnp.bfloat16):
    entries = jax.random.normal(rng, shape, jnp.float32) * width
    if len(cuts) > 0:
        entries = block_levels(rng, shape, cuts, -0.22, 0.18) * entries
    return jnp.clip(entries, min=-limit, max=limit).astype(dtype)


def setup_inputs(seed: int = 0) -> dict:
    key_of = jax.random.split(jax.random.key(seed), 9)
    return {
        "residual": bell_draw(key_of[0], (SX, SY, SZ, R, NI), 1.0, 6.0, ((0, 4), (1, 8), (2, 8))),
        "schur_inverse": bell_draw(key_of[1], (SX, SY, SZ, NI, NI), NI ** -0.5, 0.15625, ((0, 4), (1, 8), (2, 8))),
        "coarse_basis": bell_draw(key_of[2], (SX, SY, SZ, NC, NI), (4 * NC) ** -0.5, 0.25, ((0, 4), (1, 8), (2, 8))),
        "coarse_index": plant(jax.random.randint(key_of[3], (SX, SY, SZ, NC), 0, C2), jax.random.fold_in(key_of[3], 1), 0, C2 - 1).astype(jnp.int32),
        "block_slot": draw_block_slot(jax.random.fold_in(key_of[8], 71), 0),
        "group_inverse": bell_draw(key_of[5], (SX, SY, C2, C2), C2 ** -0.5, 0.25, ((0, 4), (1, 8)), jnp.float32),
        "group_restrict": bell_draw(key_of[6], (SX, SY, C2, C3), C2 ** -0.5, 0.25, ((0, 4), (1, 8)), jnp.float32),
        "top_inverse": bell_draw(key_of[7], (C3, C3), (C3 * SX * SY) ** -0.5, 0.046875, (), jnp.float32),
    }


exact_prec = lax.Precision.HIGHEST


def shift_from_lower(field, along):
    widths = [(0, 0)] * field.ndim
    widths[along] = (1, 0)
    return lax.slice_in_dim(jnp.pad(field, widths), 0, field.shape[along], axis=along)


def shift_from_upper(field, along):
    widths = [(0, 0)] * field.ndim
    widths[along] = (0, 1)
    return lax.slice_in_dim(jnp.pad(field, widths), 1, field.shape[along] + 1, axis=along)


def side_weight(length, along, lower):
    position = jnp.arange(length)
    inside = position > 0 if lower else position < length - 1
    weights = jnp.where(inside, 0.5, 1.0).astype(jnp.float32)
    shape_list = [1] * 6
    shape_list[along] = length
    return weights.reshape(shape_list)


def reference(residual, schur_inverse, coarse_basis, coarse_index, block_slot, group_inverse, group_restrict, top_inverse):
    grid_x, grid_y, grid_z = residual.shape[0], residual.shape[1], residual.shape[2]
    subdomains = grid_x * grid_y * grid_z
    rhs_count = residual.shape[3]
    columns = jnp.arange(C2).astype(jnp.int32)
    res_all = residual.reshape(subdomains, rhs_count, NI)
    inverse_all = schur_inverse.reshape(subdomains, NI, NI)
    basis_all = coarse_basis.reshape(subdomains, NC, NI)
    index_all = coarse_index.reshape(subdomains, NC).astype(jnp.int32)

    def local_terms(inputs):
        res_one, inverse_one, basis_one, index_one = inputs
        rows_float = res_one.astype(jnp.float32)
        local_sol = jnp.dot(rows_float, inverse_one.astype(jnp.float32), precision=exact_prec)
        coarse_part = jnp.dot(rows_float, basis_one.astype(jnp.float32).T, precision=exact_prec)
        onehot = (index_one[:, None] == columns[None, :]).astype(jnp.float32)
        return local_sol, jnp.dot(coarse_part, onehot, precision=exact_prec)

    local_sol, assembled = lax.map(local_terms, (res_all, inverse_all, basis_all, index_all))
    group_res = jnp.sum(assembled.reshape(grid_x, grid_y, grid_z, rhs_count, C2), axis=2)
    top_res = jnp.einsum("abrk,abkm->rm", group_res, group_restrict, precision=exact_prec)
    top_sol = jnp.dot(top_res, top_inverse, precision=exact_prec)
    group_sol = jnp.einsum("abrk,abkl->abrl", group_res, group_inverse, precision=exact_prec)
    group_sol = group_sol + jnp.einsum("rm,abkm->abrk", top_sol, group_restrict, precision=exact_prec)
    spread = jnp.broadcast_to(group_sol[:, :, None], (grid_x, grid_y, grid_z, rhs_count, C2))
    spread = spread.reshape(subdomains, rhs_count, C2)

    def finish(inputs):
        group_one, index_one, basis_one, local_one = inputs
        onehot = (index_one[:, None] == columns[None, :]).astype(jnp.float32)
        local_coarse = jnp.dot(group_one, onehot.T, precision=exact_prec).astype(jnp.bfloat16)
        prolonged = jnp.dot(local_coarse.astype(jnp.float32), basis_one.astype(jnp.float32), precision=exact_prec)
        return (local_one + prolonged).astype(jnp.bfloat16)

    update = lax.map(finish, (spread, index_all, basis_all, local_sol))
    blocks = update.reshape(grid_x, grid_y, grid_z, rhs_count, 6, FB, BW).astype(jnp.float32)
    slot_all = block_slot.reshape(grid_x, grid_y, grid_z, 6, FB).astype(jnp.int32)
    slot_onehot = (slot_all[..., None] == jnp.arange(FB).astype(jnp.int32)).astype(jnp.float32)
    slotted = jnp.einsum("xyzrfbw,xyzfbk->xyzrfkw", blocks, slot_onehot, precision=exact_prec)
    face_list = []
    for along in range(3):
        length = slotted.shape[along]
        low_face = slotted[:, :, :, :, 2 * along]
        high_face = slotted[:, :, :, :, 2 * along + 1]
        face_list.append(side_weight(length, along, True) * (low_face + shift_from_lower(high_face, along)))
        face_list.append(side_weight(length, along, False) * (high_face + shift_from_upper(low_face, along)))
    shared = jnp.stack(face_list, axis=4)
    placed = jnp.einsum("xyzrfkw,xyzfbk->xyzrfbw", shared, slot_onehot, precision=exact_prec)
    return placed.reshape(grid_x, grid_y, grid_z, rhs_count, NI).astype(jnp.bfloat16)
```

```python
import functools

import jax
import jax.numpy as jnp
from jax import lax
from jax.experimental import pallas as pl
from jax.experimental.pallas import tpu as pltpu
from jax.sharding import PartitionSpec as P

BW = 128
FACE = 256
FACES = 6
NI = 1536
NC = 128
C2 = 512
R = 512
SX, SY, SZ = 4, 8, 8
RX = R // (SX * SZ)
RZ = R // SZ
TAIL = 16
PACK = RZ + TAIL
BASE = 16

LAST = (((1,), (1,)), ((), ()))
FIRST = (((0,), (0,)), ((), ()))
f32 = jnp.float32
bf16 = jnp.bfloat16


def mm(a, b):
    return jnp.dot(a, b, preferred_element_type=f32)


def split(x):
    hi = x.astype(bf16)
    return hi, (x - hi.astype(f32)).astype(bf16)


def mm3(a, b):
    a_hi, a_lo = split(a)
    b_hi, b_lo = split(b)
    return mm(a_hi, b_hi) + (mm(a_hi, b_lo) + mm(a_lo, b_hi))


def swap_halves(x, swap):
    return jnp.where(swap, jnp.concatenate([x[:, BW:], x[:, :BW]], axis=1), x)


def call(body, out_shape, flops, size, vmem=24, **kw):
    return pl.pallas_call(
        body,
        out_shape=out_shape,
        cost_estimate=pl.CostEstimate(flops=flops, bytes_accessed=size, transcendentals=0),
        compiler_params=pltpu.CompilerParams(vmem_limit_bytes=vmem << 20),
        **kw,
    )


def whole(shape):
    return pl.BlockSpec(shape, lambda *_: (0,) * len(shape))


SMEM = pl.BlockSpec(memory_space=pltpu.SMEM)
VMEM = pl.BlockSpec(memory_space=pltpu.VMEM)


def coarse_body(idx_ref, res_ref, basis_ref, out_ref):
    step = pl.program_id(0)
    part = lax.dot_general(res_ref[...], basis_ref[...], LAST, preferred_element_type=f32)
    start = pl.multiple_of(step * RX, RX)
    out_ref[:, pl.ds(start, RX), :] = part.astype(bf16).reshape(SZ, RX, NC)

    @pl.when(step == 0)
    def _():
        idx = idx_ref[...]
        row = lax.broadcasted_iota(jnp.int32, (TAIL, NC), 0)
        digits = jnp.where(row == 0, idx >> 4, jnp.where(row == 1, idx & (BASE - 1), 0))
        digits = digits.astype(f32).astype(bf16)
        out_ref[:, RZ:, :] = jnp.broadcast_to(digits[None], (SZ, TAIL, NC))


def coarse_kernel(idx, res, basis):
    return call(
        coarse_body,
        jax.ShapeDtypeStruct((SZ, PACK, NC), bf16),
        2 * R * NI * NC,
        2 * R * NI + 2 * NC * NI,
        grid=(SX,),
        in_specs=[
            whole((1, NC)),
            pl.BlockSpec((R // SX, NI), lambda i: (i, 0)),
            whole((NC, NI)),
        ],
        out_specs=whole((SZ, PACK, NC)),
    )(idx, res, basis)


def local_body(res_ref, schur_ref, out_ref):
    out_ref[...] = mm(res_ref[...], schur_ref[...])


def local_kernel(res, schur):
    return call(
        local_body,
        jax.ShapeDtypeStruct((R, NI), f32),
        2 * R * NI * NI,
        2 * R * NI + 2 * NI * NI + 4 * R * NI,
        grid=(FACES,),
        in_specs=[whole((R, NI)), pl.BlockSpec((NI, FACE), lambda i: (0, i))],
        out_specs=pl.BlockSpec((R, FACE), lambda i: (0, i)),
    )(res, schur)


def member_onehot(pack_ref):
    digits = pack_ref[:, RZ:, :].astype(f32)
    column = lax.broadcasted_iota(jnp.int32, (C2, NC), 0).astype(f32)
    parts = []
    for c in range(SZ):
        idx = digits[c, 0:1, :] * float(BASE) + digits[c, 1:2, :]
        parts.append((column == idx).astype(bf16))
    return jnp.concatenate(parts, axis=1)


def group_body(pack_ref, restrict_ref, res_ref, top_ref):
    onehot = member_onehot(pack_ref)
    rows = jnp.concatenate([pack_ref[c, :RZ, :] for c in range(SZ)], axis=1)
    group_res = lax.dot_general(rows, onehot, LAST, preferred_element_type=f32)
    res_ref[...] = group_res
    top_ref[...] = mm3(group_res, restrict_ref[...]).astype(bf16).reshape(SX, RX, C2)


def group_kernel(pack, restrict):
    return call(
        group_body,
        (jax.ShapeDtypeStruct((RZ, C2), f32), jax.ShapeDtypeStruct((SX, RX, C2), bf16)),
        2 * RZ * C2 * (1024 + 3 * C2),
        4 * C2 * C2,
        in_specs=[VMEM] * 2,
        out_specs=(VMEM, VMEM),
    )(pack, restrict)


def back_body(pack_ref, res_ref, inv_ref, out_ref):
    onehot = member_onehot(pack_ref)
    sol = mm3(res_ref[...], inv_ref[...]).astype(bf16)
    picked = mm(sol, onehot).astype(bf16)
    for c in range(SZ):
        out_ref[c] = picked[:, c * NC : (c + 1) * NC]


def back_kernel(pack, group_res, group_inv):
    return call(
        back_body,
        jax.ShapeDtypeStruct((SZ, RZ, NC), bf16),
        2 * RZ * C2 * (1024 + 3 * C2),
        4 * C2 * C2,
        in_specs=[VMEM] * 3,
        out_specs=VMEM,
    )(pack, group_res, group_inv)


def fan_body(copies, in_ref, out_ref):
    total = jnp.sum(in_ref[...].astype(f32), axis=0).astype(bf16)
    out_ref[...] = jnp.broadcast_to(total[None], (copies,) + total.shape)


def fan_kernel(x, copies):
    n, rows, width = x.shape
    return call(
        functools.partial(fan_body, copies),
        jax.ShapeDtypeStruct((copies, rows, width), bf16),
        n * rows * width,
        2 * (n + copies) * rows * width,
        in_specs=[VMEM],
        out_specs=VMEM,
    )(x)


def face_body(slot_ref, idx_ref, back_ref, basis_ref, local_ref, restrict_ref, own_a_ref, own_k_ref, *rest):
    sends, rows_ref = rest[:FACES], rest[FACES]
    for c in range(SZ):
        for a in range(SX):
            start = (a * SZ + c) * RX
            rows_ref[start : start + RX, :] = back_ref[c, a * RX : (a + 1) * RX, :]
    rows = rows_ref[...]
    column = lax.broadcasted_iota(jnp.int32, (C2, NC), 0)
    onehot = (column == idx_ref[...]).astype(bf16)
    r_hi, r_lo = split(restrict_ref[...])
    m_hi = lax.dot_general(r_hi, onehot, FIRST, preferred_element_type=f32).astype(bf16)
    m_lo = lax.dot_general(r_lo, onehot, FIRST, preferred_element_type=f32).astype(bf16)
    for f in range(FACES):
        cols = slice(f * FACE, (f + 1) * FACE)
        swap = slot_ref[0, 2 * f] == 1
        basis = basis_ref[:, cols]
        own_a = local_ref[:, cols] + mm(rows, basis)
        own_k = (mm(m_hi, basis) + mm(m_lo, basis)).astype(bf16)
        own_a_ref[:, cols] = own_a
        own_k_ref[:, cols] = own_k
        sends[f][:C2, :] = swap_halves(own_k.astype(f32), swap).astype(bf16)
        sends[f][C2:, :] = swap_halves(own_a, swap).astype(bf16)


def face_kernel(slots, idx, back, basis, local, restrict):
    return call(
        face_body,
        (
            jax.ShapeDtypeStruct((R, NI), f32),
            jax.ShapeDtypeStruct((C2, NI), bf16),
        )
        + (jax.ShapeDtypeStruct((C2 + R, FACE), bf16),) * FACES,
        2 * R * NC * NI * 3,
        8 * R * NI,
        in_specs=[SMEM] + [VMEM] * 5,
        out_specs=(VMEM,) * (2 + FACES),
        scratch_shapes=[pltpu.VMEM((R, NC), bf16)],
    )(slots, idx, back, basis, local, restrict)


def blend_body(slot_ref, weight_ref, a_ref, k_ref, inv_ref, *rest):
    gots, out_a_ref, out_w_ref = rest[:FACES], rest[FACES], rest[FACES + 1]
    i_hi, i_lo = split(inv_ref[...])
    for f in range(FACES):
        cols = slice(f * FACE, (f + 1) * FACE)
        swap = slot_ref[0, 2 * f] == 1
        weight = weight_ref[0, f]
        got_k = swap_halves(gots[f][:C2, :].astype(f32), swap)
        got_a = swap_halves(gots[f][C2:, :].astype(f32), swap)
        k = (weight * (k_ref[:, cols].astype(f32) + got_k)).astype(bf16)
        out_a_ref[:, cols] = weight * (a_ref[:, cols] + got_a)
        out_w_ref[:, cols] = (mm(i_hi, k) + mm(i_lo, k)).astype(bf16)


def blend_kernel(slots, weights, own_a, own_k, inv, gots):
    return call(
        blend_body,
        (jax.ShapeDtypeStruct((R, NI), f32), jax.ShapeDtypeStruct((C2, NI), bf16)),
        2 * C2 * C2 * NI * 2,
        12 * R * NI,
        vmem=32,
        in_specs=[SMEM] * 2 + [VMEM] * (3 + FACES),
        out_specs=(VMEM, VMEM),
    )(slots, weights, own_a, own_k, inv, *gots)


def last_body(top_ref, w_ref, a_ref, out_ref):
    out_ref[...] = (a_ref[...] + mm(top_ref[...], w_ref[...])).astype(bf16)


def last_kernel(top, w, a):
    rows = 128
    return call(
        last_body,
        jax.ShapeDtypeStruct((R, NI), bf16),
        2 * R * C2 * NI,
        8 * R * NI,
        grid=(R // rows,),
        in_specs=[
            pl.BlockSpec((rows, C2), lambda i: (i, 0)),
            whole((C2, NI)),
            pl.BlockSpec((rows, NI), lambda i: (i, 0)),
        ],
        out_specs=pl.BlockSpec((rows, NI), lambda i: (i, 0)),
    )(top, w, a)


def per_device(
    residual,
    schur_inverse,
    coarse_basis,
    coarse_index,
    block_slot,
    group_inverse,
    group_restrict,
    top_inverse,
):
    res = residual[0, 0, 0]
    schur = schur_inverse[0, 0, 0]
    basis = coarse_basis[0, 0, 0]
    idx = coarse_index.reshape(1, NC)
    slots = block_slot.reshape(1, 2 * FACES)
    group_inv = group_inverse[0, 0]
    restrict = group_restrict[0, 0]

    pack = coarse_kernel(idx, res, basis)
    pack = lax.all_to_all(pack, "gz", 0, 0)
    local = local_kernel(res, schur)
    group_res, part = group_kernel(pack, restrict)
    part = lax.all_to_all(part, "gx", 0, 0)
    back = back_kernel(pack, group_res, group_inv)
    back = lax.all_to_all(back, "gz", 0, 0)
    part = lax.all_to_all(fan_kernel(part, SY), "gy", 0, 0)
    own_a, own_k, *sends = face_kernel(slots, idx, back, basis, local, restrict)
    top = lax.all_to_all(fan_kernel(part, SX * SZ), ("gx", "gz"), 0, 0).reshape(R, C2)

    gots, weights = [], []
    for axis, count, f in (("gx", SX, 0), ("gy", SY, 2), ("gz", SZ, 4)):
        up = [(i, i + 1) for i in range(count - 1)]
        down = [(i + 1, i) for i in range(count - 1)]
        place = lax.axis_index(axis)
        gots.append(lax.ppermute(sends[f + 1], axis, up))
        gots.append(lax.ppermute(sends[f], axis, down))
        weights.append(jnp.where(place > 0, 0.5, 1.0).astype(f32))
        weights.append(jnp.where(place < count - 1, 0.5, 1.0).astype(f32))
    weights = jnp.stack(weights).reshape(1, FACES)
    a, w = blend_kernel(slots, weights, own_a, own_k, top_inverse, gots)
    return last_kernel(top, w, a).reshape(1, 1, 1, R, NI)


def solution(mesh):
    return jax.shard_map(
        per_device,
        mesh=mesh,
        in_specs=(
            P("gx", "gy", "gz", None, None),
            P("gx", "gy", "gz", None, None),
            P("gx", "gy", "gz", None, None),
            P("gx", "gy", "gz", None),
            P("gx", "gy", "gz", None),
            P("gx", "gy", None, None),
            P("gx", "gy", None, None),
            P(),
        ),
        out_specs=P("gx", "gy", "gz", None, None),
        check_vma=False,
    )
```

```python
import functools

import jax
import jax.numpy as jnp
from jax import lax
from jax.experimental import pallas as pl
from jax.experimental.pallas import tpu as pltpu
from jax.sharding import PartitionSpec as P

BW = 128
FACE = 256
FACES = 6
NI = 1536
NC = 128
C2 = 512
R = 512
SX, SY, SZ = 4, 8, 8
RX = R // (SX * SZ)
RZ = R // SZ
TAIL = 16
PACK = RZ + TAIL
BASE = 16
COST = 1024
BIG = 58
SMALL = 6
CHIPS = SZ // 2

LAST = (((1,), (1,)), ((), ()))
FIRST = (((0,), (0,)), ((), ()))
f32 = jnp.float32
bf16 = jnp.bfloat16


def mm(a, b):
    return jnp.dot(a, b, preferred_element_type=f32)


def split(x):
    hi = x.astype(bf16)
    return hi, (x - hi.astype(f32)).astype(bf16)


def mm3(a, b):
    a_hi, a_lo = split(a)
    b_hi, b_lo = split(b)
    return mm(a_hi, b_hi) + (mm(a_hi, b_lo) + mm(a_lo, b_hi))


def swap_halves(x, swap):
    return jnp.where(swap, jnp.concatenate([x[:, BW:], x[:, :BW]], axis=1), x)


def call(body, out_shape, flops, size, vmem, **kw):
    return pl.pallas_call(
        body,
        out_shape=out_shape,
        cost_estimate=pl.CostEstimate(flops=COST, bytes_accessed=COST, transcendentals=0),
        compiler_params=pltpu.CompilerParams(vmem_limit_bytes=vmem << 20),
        **kw,
    )


SMEM = pl.BlockSpec(memory_space=pltpu.SMEM)
VMEM = pl.BlockSpec(memory_space=pltpu.VMEM)
HBM = pl.BlockSpec(memory_space=pltpu.HBM)
DMA = pltpu.SemaphoreType.DMA


def started(pairs, sems):
    copies = []
    for i, (src, dst) in enumerate(pairs):
        copies.append(pltpu.make_async_copy(src, dst, sems.at[i]))
        copies[-1].start()
    return copies


def face_cols(f):
    return slice(f * FACE, (f + 1) * FACE)


def coarse_body(idx_hbm, res_hbm, basis_hbm, out_ref, res_ref, idx_ref, basis_ref, sems):
    rows = R // SX
    pairs = [(basis_hbm, basis_ref)]
    for a in range(SX):
        part = pl.ds(a * rows, rows)
        pairs.append((res_hbm.at[part], res_ref.at[part]))
    pairs.append((idx_hbm, idx_ref))
    copies = started(pairs, sems)
    copies[0].wait()
    for a in range(SX):
        copies[1 + a].wait()
        part = lax.dot_general(
            res_ref[a * rows : (a + 1) * rows, :], basis_ref[...], LAST, preferred_element_type=f32
        )
        out_ref[:, a * RX : (a + 1) * RX, :] = part.astype(bf16).reshape(SZ, RX, NC)
    copies[1 + SX].wait()
    idx = idx_ref[...]
    row = lax.broadcasted_iota(jnp.int32, (TAIL, NC), 0)
    digits = jnp.where(row == 0, idx >> 4, jnp.where(row == 1, idx & (BASE - 1), 0))
    digits = digits.astype(f32).astype(bf16)
    out_ref[:, RZ:, :] = jnp.broadcast_to(digits[None], (SZ, TAIL, NC))


def coarse_kernel(idx, res, basis):
    return call(
        coarse_body,
        (jax.ShapeDtypeStruct((SZ, PACK, NC), bf16), jax.ShapeDtypeStruct((R, NI), bf16)),
        0,
        0,
        vmem=BIG,
        in_specs=[HBM] * 3,
        out_specs=(VMEM, VMEM),
        scratch_shapes=[
            pltpu.VMEM((1, NC), jnp.int32),
            pltpu.VMEM((NC, NI), bf16),
            DMA((2 + SX,)),
        ],
    )(idx, res, basis)


def local_body(res_ref, schur_ref, out_ref):
    for f in range(FACES):
        out_ref[f] = mm(res_ref[...], schur_ref[:, face_cols(f)])


def local_kernel(res, schur):
    return call(
        local_body,
        jax.ShapeDtypeStruct((FACES, R, FACE), f32),
        0,
        0,
        vmem=SMALL,
        in_specs=[VMEM] * 2,
        out_specs=VMEM,
    )(res, schur)


def member_onehot(pack_ref):
    digits = pack_ref[:, RZ:, :].astype(f32)
    column = lax.broadcasted_iota(jnp.int32, (C2, NC), 0).astype(f32)
    parts = []
    for c in range(SZ):
        idx = digits[c, 0:1, :] * float(BASE) + digits[c, 1:2, :]
        parts.append((column == idx).astype(bf16))
    return jnp.concatenate(parts, axis=1)


def group_body(pack_ref, restrict_ref, res_ref, top_ref):
    onehot = member_onehot(pack_ref)
    rows = jnp.concatenate([pack_ref[c, :RZ, :] for c in range(SZ)], axis=1)
    group_res = lax.dot_general(rows, onehot, LAST, preferred_element_type=f32)
    res_ref[...] = group_res
    top_ref[...] = mm3(group_res, restrict_ref[...]).astype(bf16)


def group_kernel(pack, restrict):
    return call(
        group_body,
        (jax.ShapeDtypeStruct((RZ, C2), f32), jax.ShapeDtypeStruct((RZ, C2), bf16)),
        0,
        0,
        vmem=8,
        in_specs=[VMEM] * 2,
        out_specs=(VMEM, VMEM),
    )(pack, restrict)


def map_body(top_inv_ref, restrict_ref, hi_ref, lo_ref):
    t_hi, t_lo = split(top_inv_ref[...])
    r_hi, r_lo = split(restrict_ref[...])
    back = functools.partial(lax.dot_general, dimension_numbers=LAST, preferred_element_type=f32)
    both = back(t_hi, r_hi) + (back(t_hi, r_lo) + back(t_lo, r_hi))
    hi_ref[...], lo_ref[...] = split(both)


def map_kernel(top_inv, restrict):
    return call(
        map_body,
        (jax.ShapeDtypeStruct((C2, C2), bf16),) * 2,
        0,
        0,
        vmem=SMALL,
        in_specs=[VMEM] * 2,
        out_specs=(VMEM,) * 2,
    )(top_inv, restrict)


def own_body(res_ref, group_inv_ref, own_ref):
    own_ref[...] = mm3(res_ref[...], group_inv_ref[...])


def own_kernel(group_res, group_inv):
    return call(
        own_body,
        jax.ShapeDtypeStruct((RZ, C2), f32),
        0,
        0,
        vmem=SMALL,
        in_specs=[VMEM] * 2,
        out_specs=VMEM,
    )(group_res, group_inv)


def solve_body(pack_ref, own_ref, hi_ref, lo_ref, *refs):
    parts, out_ref = refs[:-1], refs[-1]
    onehot = member_onehot(pack_ref)
    top_res = sum(p[...].astype(f32) for p in parts)
    t_hi, t_lo = split(top_res)
    sol = own_ref[...] + mm(t_hi, hi_ref[...]) + (mm(t_hi, lo_ref[...]) + mm(t_lo, hi_ref[...]))
    picked = mm(sol.astype(bf16), onehot).astype(bf16)
    for c in range(SZ):
        out_ref[c] = picked[:, c * NC : (c + 1) * NC]


def solve_kernel(pack, own, map_hi, map_lo, parts):
    return call(
        solve_body,
        jax.ShapeDtypeStruct((SZ, RZ, NC), bf16),
        0,
        0,
        vmem=8,
        in_specs=[VMEM] * (4 + len(parts)),
        out_specs=VMEM,
    )(pack, own, map_hi, map_lo, *parts)


def sum_body(*refs):
    refs[-1][...] = sum(r[...].astype(f32) for r in refs[:-1]).astype(bf16)


def sum_kernel(parts):
    return call(
        sum_body,
        jax.ShapeDtypeStruct((RZ, C2), bf16),
        0,
        0,
        vmem=4,
        in_specs=[VMEM] * len(parts),
        out_specs=VMEM,
    )(*parts)


def send_face(meta_ref, e):
    odd = meta_ref[0, 18 + e // 2]
    return e // 2 * 2 + (odd if e % 2 else 1 - odd)


def update_body(meta_ref, back_ref, basis_ref, local_ref, *refs):
    sends, rows_ref = refs[:FACES], refs[FACES]
    for c in range(SZ):
        for a in range(SX):
            start = (a * SZ + c) * RX
            rows_ref[start : start + RX, :] = back_ref[c, a * RX : (a + 1) * RX, :]
    rows = rows_ref[...]
    for e in range(FACES):
        f = send_face(meta_ref, e)
        cols = pl.ds(pl.multiple_of(f * FACE, FACE), FACE)
        update = local_ref[f] + mm(rows, basis_ref[:, cols])
        sends[e][...] = swap_halves(update, meta_ref[0, 2 * f] == 1).astype(bf16)


def update_kernel(meta, back, basis, local):
    return call(
        update_body,
        (jax.ShapeDtypeStruct((R, FACE), bf16),) * FACES,
        0,
        0,
        vmem=SMALL,
        in_specs=[SMEM] + [VMEM] * 3,
        out_specs=(VMEM,) * FACES,
        scratch_shapes=[pltpu.VMEM((R, NC), bf16)],
    )(meta, back, basis, local)


def last_body(meta_ref, *refs):
    sends, gots = refs[:FACES], refs[FACES : 2 * FACES]
    out_hbm, out_ref, out_sems = refs[2 * FACES :]
    outs = []
    for e in range(FACES):
        f = send_face(meta_ref, e)
        cols = pl.ds(pl.multiple_of(f * FACE, FACE), FACE)
        weight = jnp.where(meta_ref[0, 12 + f] == 1, 0.5, 1.0).astype(f32)
        both = weight * (sends[e][...].astype(f32) + gots[e][...].astype(f32))
        out_ref[e] = swap_halves(both, meta_ref[0, 2 * f] == 1).astype(bf16)
        outs += started([(out_ref.at[e], out_hbm.at[:, cols])], out_sems.at[pl.ds(e, 1)])
    for c in outs:
        c.wait()


def last_kernel(meta, sends, gots):
    return call(
        last_body,
        jax.ShapeDtypeStruct((R, NI), bf16),
        0,
        0,
        vmem=SMALL,
        in_specs=[SMEM] + [VMEM] * (2 * FACES),
        out_specs=HBM,
        scratch_shapes=[pltpu.VMEM((FACES, R, FACE), bf16), DMA((FACES,))],
    )(meta, *sends, *gots)


def ring(count, d):
    return [(i, (i + d) % count) for i in range(count)]


def after(x, *others):
    return lax.optimization_barrier((x,) + others)[0]


def per_device(
    residual,
    schur_inverse,
    coarse_basis,
    coarse_index,
    block_slot,
    group_inverse,
    group_restrict,
    top_inverse,
):
    res = residual[0, 0, 0]
    schur = schur_inverse[0, 0, 0]
    basis = coarse_basis[0, 0, 0]
    idx = coarse_index.reshape(1, NC)
    group_inv = group_inverse[0, 0]
    restrict = group_restrict[0, 0]
    place = [lax.axis_index(axis) for axis in ("gx", "gy", "gz")]
    facts = []
    for at, count in zip(place, (SX, SY, SZ)):
        facts += [at > 0, at < count - 1]
    facts += [at % 2 for at in place]
    facts = jnp.stack([jnp.asarray(v, jnp.int32) for v in facts])
    meta = jnp.concatenate([block_slot.reshape(2 * FACES), facts]).reshape(1, -1)

    pack, res = coarse_kernel(idx, res, basis)
    local = local_kernel(res, schur)
    pack = after(lax.all_to_all(pack, "gz", 0, 0), local)
    group_res, part = group_kernel(pack, restrict)
    top_map = map_kernel(top_inverse, after(restrict, part))
    own = own_kernel(group_res, group_inv)
    gots = [part] + [lax.ppermute(part, "gx", [(i, i ^ d) for i in range(SX)]) for d in (1, 3, 2)]
    part = sum_kernel(lax.optimization_barrier((*gots, *top_map))[:SX])
    got = after(lax.ppermute(part, "gy", [(i, i ^ 1) for i in range(SY)]), own)
    part = sum_kernel([part, got])
    part = sum_kernel([part, lax.ppermute(part, "gy", [(i, i ^ 2) for i in range(SY)])])
    parts = [part, lax.ppermute(part, "gy", [(i, SY - 1 - i) for i in range(SY)])]
    back = solve_kernel(pack, own, *top_map, parts)
    back = lax.all_to_all(back, "gz", 0, 0)
    sends = update_kernel(meta, back, basis, local)
    gots = []
    for axis, count, e in (("gx", SX, 0), ("gy", SY, 2), ("gz", SZ, 4)):
        near = [(i, i + 1) for i in range(0, count, 2)]
        far = [(i, i + 1) for i in range(1, count - 1, 2)]
        for f, pairs in ((e, near), (e + 1, far)):
            gots.append(lax.ppermute(sends[f], axis, pairs + [(j, i) for i, j in pairs]))
    return last_kernel(meta, sends, gots).reshape(1, 1, 1, R, NI)


def solution(mesh):
    return jax.shard_map(
        per_device,
        mesh=mesh,
        in_specs=(
            P("gx", "gy", "gz", None, None),
            P("gx", "gy", "gz", None, None),
            P("gx", "gy", "gz", None, None),
            P("gx", "gy", "gz", None),
            P("gx", "gy", "gz", None),
            P("gx", "gy", None, None),
            P("gx", "gy", None, None),
            P(),
        ),
        out_specs=P("gx", "gy", "gz", None, None),
        check_vma=False,
    )
```

```python
import functools

import jax
import jax.numpy as jnp
from jax import lax
from jax.experimental import pallas as pl
from jax.experimental.pallas import tpu as pltpu
from jax.sharding import PartitionSpec as P

BW = 128
FACE = 256
FACES = 6
NI = 1536
NC = 128
C2 = 512
R = 512
SX, SY, SZ = 4, 8, 8
RX = R // (SX * SZ)
RZ = R // SZ
TAIL = 16
PACK = RZ + TAIL
BASE = 16
COST = 1024
BIG = 58
SMALL = 6
ORDER = (0, 2, 1, 3, 5, 4)
CHIPS = SZ // 2

LAST = (((1,), (1,)), ((), ()))
FIRST = (((0,), (0,)), ((), ()))
f32 = jnp.float32
bf16 = jnp.bfloat16


def mm(a, b):
    return jnp.dot(a, b, preferred_element_type=f32)


def split(x):
    hi = x.astype(bf16)
    return hi, (x - hi.astype(f32)).astype(bf16)


def mm3(a, b):
    a_hi, a_lo = split(a)
    b_hi, b_lo = split(b)
    return mm(a_hi, b_hi) + (mm(a_hi, b_lo) + mm(a_lo, b_hi))


def swap_halves(x, swap):
    return jnp.where(swap, jnp.concatenate([x[:, BW:], x[:, :BW]], axis=1), x)


def call(body, out_shape, flops, size, vmem, **kw):
    return pl.pallas_call(
        body,
        out_shape=out_shape,
        cost_estimate=pl.CostEstimate(flops=COST, bytes_accessed=COST, transcendentals=0),
        compiler_params=pltpu.CompilerParams(vmem_limit_bytes=vmem << 20),
        **kw,
    )


SMEM = pl.BlockSpec(memory_space=pltpu.SMEM)
VMEM = pl.BlockSpec(memory_space=pltpu.VMEM)
ANY = pl.BlockSpec(memory_space=pl.ANY)
HBM = pl.BlockSpec(memory_space=pltpu.HBM)
DMA = pltpu.SemaphoreType.DMA


def started(pairs, sems):
    copies = []
    for i, (src, dst) in enumerate(pairs):
        copies.append(pltpu.make_async_copy(src, dst, sems.at[i]))
        copies[-1].start()
    return copies


def face_cols(f):
    return slice(f * FACE, (f + 1) * FACE)


def coarse_body(idx_hbm, res_hbm, basis_hbm, out_ref, idx_ref, res_ref, basis_ref, sems):
    rows = R // SX
    pairs = [(basis_hbm, basis_ref)]
    for a in range(SX):
        part = pl.ds(a * rows, rows)
        pairs.append((res_hbm.at[part], res_ref.at[part]))
    pairs.append((idx_hbm, idx_ref))
    copies = started(pairs, sems)
    copies[0].wait()
    for a in range(SX):
        copies[1 + a].wait()
        part = lax.dot_general(
            res_ref[a * rows : (a + 1) * rows, :], basis_ref[...], LAST, preferred_element_type=f32
        )
        out_ref[:, a * RX : (a + 1) * RX, :] = part.astype(bf16).reshape(SZ, RX, NC)
    copies[1 + SX].wait()
    idx = idx_ref[...]
    row = lax.broadcasted_iota(jnp.int32, (TAIL, NC), 0)
    digits = jnp.where(row == 0, idx >> 4, jnp.where(row == 1, idx & (BASE - 1), 0))
    digits = digits.astype(f32).astype(bf16)
    out_ref[:, RZ:, :] = jnp.broadcast_to(digits[None], (SZ, TAIL, NC))


def coarse_kernel(idx, res, basis):
    return call(
        coarse_body,
        jax.ShapeDtypeStruct((SZ, PACK, NC), bf16),
        0,
        0,
        vmem=BIG,
        in_specs=[HBM] * 3,
        out_specs=VMEM,
        scratch_shapes=[
            pltpu.VMEM((1, NC), jnp.int32),
            pltpu.VMEM((R, NI), bf16),
            pltpu.VMEM((NC, NI), bf16),
            DMA((2 + SX,)),
        ],
    )(idx, res, basis)


def local_body(res_ref, schur_ref, _, out_ref):
    for f in range(FACES):
        out_ref[f] = mm(res_ref[...], schur_ref[:, face_cols(f)])


def local_kernel(res, schur, earlier):
    return call(
        local_body,
        jax.ShapeDtypeStruct((FACES, R, FACE), f32),
        0,
        0,
        vmem=SMALL,
        in_specs=[VMEM, VMEM, ANY],
        out_specs=VMEM,
    )(res, schur, earlier)


def member_onehot(pack_ref):
    digits = pack_ref[:, RZ:, :].astype(f32)
    column = lax.broadcasted_iota(jnp.int32, (C2, NC), 0).astype(f32)
    parts = []
    for c in range(SZ):
        idx = digits[c, 0:1, :] * float(BASE) + digits[c, 1:2, :]
        parts.append((column == idx).astype(bf16))
    return jnp.concatenate(parts, axis=1)


def group_body(pack_ref, restrict_ref, res_ref, top_ref):
    onehot = member_onehot(pack_ref)
    rows = jnp.concatenate([pack_ref[c, :RZ, :] for c in range(SZ)], axis=1)
    group_res = lax.dot_general(rows, onehot, LAST, preferred_element_type=f32)
    res_ref[...] = group_res
    top_ref[...] = mm3(group_res, restrict_ref[...]).astype(bf16)


def group_kernel(pack, restrict):
    return call(
        group_body,
        (jax.ShapeDtypeStruct((RZ, C2), f32), jax.ShapeDtypeStruct((RZ, C2), bf16)),
        0,
        0,
        vmem=8,
        in_specs=[VMEM] * 2,
        out_specs=(VMEM, VMEM),
    )(pack, restrict)


def map_body(top_hbm, restrict_hbm, _, hi_hbm, lo_hbm, top_ref, restrict_ref, hi_ref, lo_ref, sems):
    for c in started([(top_hbm, top_ref), (restrict_hbm, restrict_ref)], sems.at[pl.ds(0, 2)]):
        c.wait()
    t_hi, t_lo = split(top_ref[...])
    r_hi, r_lo = split(restrict_ref[...])
    back = functools.partial(lax.dot_general, dimension_numbers=LAST, preferred_element_type=f32)
    both = back(t_hi, r_hi) + (back(t_hi, r_lo) + back(t_lo, r_hi))
    hi_ref[...], lo_ref[...] = split(both)
    for c in started([(hi_ref, hi_hbm), (lo_ref, lo_hbm)], sems.at[pl.ds(2, 2)]):
        c.wait()


def map_kernel(top_inv, restrict, earlier):
    return call(
        map_body,
        (jax.ShapeDtypeStruct((C2, C2), bf16),) * 2,
        0,
        0,
        vmem=BIG,
        in_specs=[HBM, HBM, ANY],
        out_specs=(HBM, HBM),
        scratch_shapes=[
            pltpu.VMEM((C2, C2), f32),
            pltpu.VMEM((C2, C2), f32),
            pltpu.VMEM((C2, C2), bf16),
            pltpu.VMEM((C2, C2), bf16),
            DMA((4,)),
        ],
    )(top_inv, restrict, earlier)


def own_body(res_ref, group_inv_ref, own_ref):
    own_ref[...] = mm3(res_ref[...], group_inv_ref[...])


def own_kernel(group_res, group_inv):
    return call(
        own_body,
        jax.ShapeDtypeStruct((RZ, C2), f32),
        0,
        0,
        vmem=SMALL,
        in_specs=[VMEM] * 2,
        out_specs=VMEM,
    )(group_res, group_inv)


def solve_body(pack_ref, own_ref, hi_ref, lo_ref, *refs):
    parts, out_ref = refs[:-1], refs[-1]
    onehot = member_onehot(pack_ref)
    top_res = sum(p[...].astype(f32) for p in parts)
    t_hi, t_lo = split(top_res)
    sol = own_ref[...] + mm(t_hi, hi_ref[...]) + (mm(t_hi, lo_ref[...]) + mm(t_lo, hi_ref[...]))
    picked = mm(sol.astype(bf16), onehot).astype(bf16)
    for c in range(SZ):
        out_ref[c] = picked[:, c * NC : (c + 1) * NC]


def solve_kernel(pack, own, map_hi, map_lo, parts):
    return call(
        solve_body,
        jax.ShapeDtypeStruct((SZ, RZ, NC), bf16),
        0,
        0,
        vmem=8,
        in_specs=[VMEM] * (4 + len(parts)),
        out_specs=VMEM,
    )(pack, own, map_hi, map_lo, *parts)


def sum_body(count, *refs):
    refs[-1][...] = sum(r[...].astype(f32) for r in refs[:count]).astype(bf16)


def sum_kernel(parts, *earlier):
    return call(
        functools.partial(sum_body, len(parts)),
        jax.ShapeDtypeStruct((RZ, C2), bf16),
        0,
        0,
        vmem=4,
        in_specs=[VMEM] * len(parts) + [ANY] * len(earlier),
        out_specs=VMEM,
    )(*parts, *earlier)


def send_face(meta_ref, e):
    odd = meta_ref[0, 18 + e // 2]
    return e // 2 * 2 + (odd if e % 2 else 1 - odd)


def face_update(meta_ref, e, rows, basis_ref, local_ref, send_ref):
    f = send_face(meta_ref, e)
    cols = pl.ds(pl.multiple_of(f * FACE, FACE), FACE)
    update = local_ref[f] + mm(rows, basis_ref[:, cols])
    send_ref[...] = swap_halves(update, meta_ref[0, 2 * f] == 1).astype(bf16)


def update_body(meta_ref, back_ref, basis_ref, local_ref, *refs):
    rows_ref = refs[FACES]
    for c in range(SZ):
        for a in range(SX):
            start = (a * SZ + c) * RX
            rows_ref[start : start + RX, :] = back_ref[c, a * RX : (a + 1) * RX, :]
    rows = rows_ref[...]
    for e, send_ref in zip(ORDER, refs):
        f = send_face(meta_ref, e)
        cols = pl.ds(pl.multiple_of(f * FACE, FACE), FACE)
        update = local_ref[f] + mm(rows, basis_ref[:, cols])
        send_ref[...] = swap_halves(update, meta_ref[0, 2 * f] == 1).astype(bf16)


def update_kernel(meta, back, basis, local):
    return call(
        update_body,
        (jax.ShapeDtypeStruct((R, FACE), bf16),) * FACES,
        0,
        0,
        vmem=SMALL,
        in_specs=[SMEM] + [VMEM] * 3,
        out_specs=(VMEM,) * FACES,
        scratch_shapes=[pltpu.VMEM((R, NC), bf16)],
    )(meta, back, basis, local)


def last_body(meta_ref, *refs):
    out_hbm, out_ref, out_sems = refs[-3:]
    outs = []
    for i, e in enumerate(ORDER):
        f = send_face(meta_ref, e)
        cols = pl.ds(pl.multiple_of(f * FACE, FACE), FACE)
        shared = meta_ref[0, 12 + f] == 1
        own, got = refs[i][...].astype(f32), refs[FACES + i][...].astype(f32)
        both = jnp.where(shared, 0.5 * (own + got), own)
        out_ref[i] = swap_halves(both, meta_ref[0, 2 * f] == 1).astype(bf16)
        outs += started([(out_ref.at[i], out_hbm.at[:, cols])], out_sems.at[pl.ds(i, 1)])
    for c in outs:
        c.wait()


def last_kernel(meta, sends, gots):
    return call(
        last_body,
        jax.ShapeDtypeStruct((R, NI), bf16),
        0,
        0,
        vmem=SMALL,
        in_specs=[SMEM] + [VMEM] * (2 * FACES),
        out_specs=HBM,
        scratch_shapes=[pltpu.VMEM((FACES, R, FACE), bf16), DMA((FACES,))],
    )(meta, *sends, *gots)


def ring(count, d):
    return [(i, (i + d) % count) for i in range(count)]


def per_device(
    residual,
    schur_inverse,
    coarse_basis,
    coarse_index,
    block_slot,
    group_inverse,
    group_restrict,
    top_inverse,
):
    res = residual[0, 0, 0]
    schur = schur_inverse[0, 0, 0]
    basis = coarse_basis[0, 0, 0]
    idx = coarse_index.reshape(1, NC)
    group_inv = group_inverse[0, 0]
    restrict = group_restrict[0, 0]
    place = [lax.axis_index(axis) for axis in ("gx", "gy", "gz")]
    facts = []
    for at, count in zip(place, (SX, SY, SZ)):
        facts += [at > 0, at < count - 1]
    facts += [at % 2 for at in place]
    facts = jnp.stack([jnp.asarray(v, jnp.int32) for v in facts])
    meta = jnp.concatenate([block_slot.reshape(2 * FACES), facts]).reshape(1, -1)

    pack = coarse_kernel(idx, res, basis)
    top_map = map_kernel(top_inverse, restrict, pack)
    pack = lax.optimization_barrier((lax.all_to_all(pack, "gz", 0, 0), top_map[0]))[0]
    group_res, part = group_kernel(pack, restrict)
    own = own_kernel(group_res, group_inv)
    gots = [part] + [lax.ppermute(part, "gx", [(i, i ^ d) for i in range(SX)]) for d in (1, 3, 2)]
    part = sum_kernel(gots)
    gots = [part] + [lax.ppermute(part, "gy", [(i, i ^ d) for i in range(SY)]) for d in (1, 3, 2)]
    part = sum_kernel(gots, own)
    parts = [part, lax.ppermute(part, "gy", [(i, SY - 1 - i) for i in range(SY)])]
    back = solve_kernel(pack, own, *top_map, parts)
    local = local_kernel(res, schur, back)
    back = lax.all_to_all(back, "gz", 0, 0)
    sends = update_kernel(meta, back, basis, local)
    gots = []
    for e, send in zip(ORDER, sends):
        axis, count = (("gx", SX), ("gy", SY), ("gz", SZ))[e // 2]
        pairs = [(i, (i + 1) % count) for i in range(e % 2, count, 2)]
        gots.append(lax.ppermute(send, axis, pairs + [(j, i) for i, j in pairs]))
    return last_kernel(meta, sends, gots).reshape(1, 1, 1, R, NI)


def solution(mesh):
    return jax.shard_map(
        per_device,
        mesh=mesh,
        in_specs=(
            P("gx", "gy", "gz", None, None),
            P("gx", "gy", "gz", None, None),
            P("gx", "gy", "gz", None, None),
            P("gx", "gy", "gz", None),
            P("gx", "gy", "gz", None),
            P("gx", "gy", None, None),
            P("gx", "gy", None, None),
            P(),
        ),
        out_specs=P("gx", "gy", "gz", None, None),
        check_vma=False,
    )
```

```python
import functools

import jax
import jax.numpy as jnp
from jax import lax
from jax.experimental import pallas as pl
from jax.experimental.pallas import tpu as pltpu
from jax.sharding import PartitionSpec as P

BW = 128
FACE = 256
FACES = 6
NI = 1536
NC = 128
C2 = 512
R = 512
SX, SY, SZ = 4, 8, 8
RX = R // (SX * SZ)
RZ = R // SZ
TAIL = 16
PACK = RZ + TAIL
BASE = 16
COST = 1024
BIG = 58
SMALL = 6
SLOTS = ((0, True), (1, True), (0, False), (1, False), (2, False), (2, True))
CHIPS = SZ // 2

LAST = (((1,), (1,)), ((), ()))
FIRST = (((0,), (0,)), ((), ()))
f32 = jnp.float32
bf16 = jnp.bfloat16


def mm(a, b):
    return jnp.dot(a, b, preferred_element_type=f32)


def split(x):
    hi = x.astype(bf16)
    return hi, (x - hi.astype(f32)).astype(bf16)


def mm3(a, b):
    a_hi, a_lo = split(a)
    b_hi, b_lo = split(b)
    return mm(a_hi, b_hi) + (mm(a_hi, b_lo) + mm(a_lo, b_hi))


def block_cols(block):
    return pl.ds(pl.multiple_of(block * BW, BW), BW)


def call(body, out_shape, flops, size, vmem, **kw):
    return pl.pallas_call(
        body,
        out_shape=out_shape,
        cost_estimate=pl.CostEstimate(flops=COST, bytes_accessed=COST, transcendentals=0),
        compiler_params=pltpu.CompilerParams(vmem_limit_bytes=vmem << 20),
        **kw,
    )


SMEM = pl.BlockSpec(memory_space=pltpu.SMEM)
VMEM = pl.BlockSpec(memory_space=pltpu.VMEM)
ANY = pl.BlockSpec(memory_space=pl.ANY)
HBM = pl.BlockSpec(memory_space=pltpu.HBM)
DMA = pltpu.SemaphoreType.DMA


def started(pairs, sems):
    copies = []
    for i, (src, dst) in enumerate(pairs):
        copies.append(pltpu.make_async_copy(src, dst, sems.at[i]))
        copies[-1].start()
    return copies


def face_cols(f):
    return slice(f * FACE, (f + 1) * FACE)


def coarse_body(idx_hbm, res_hbm, basis_hbm, out_ref, idx_ref, res_ref, basis_ref, sems):
    copies = started([(idx_hbm, idx_ref), (basis_hbm, basis_ref), (res_hbm, res_ref)], sems)
    for c in copies:
        c.wait()
    part = lax.dot_general(res_ref[...], basis_ref[...], LAST, preferred_element_type=f32)
    part = part.astype(bf16).reshape(SX, SZ, RX, NC)
    for a in range(SX):
        out_ref[:, a * RX : (a + 1) * RX, :] = part[a]
    idx = idx_ref[...]
    row = lax.broadcasted_iota(jnp.int32, (TAIL, NC), 0)
    digits = jnp.where(row == 0, idx >> 4, jnp.where(row == 1, idx & (BASE - 1), 0))
    digits = digits.astype(f32).astype(bf16)
    out_ref[:, RZ:, :] = jnp.broadcast_to(digits[None], (SZ, TAIL, NC))


def coarse_kernel(idx, res, basis):
    return call(
        coarse_body,
        jax.ShapeDtypeStruct((SZ, PACK, NC), bf16),
        0,
        0,
        vmem=BIG,
        in_specs=[HBM] * 3,
        out_specs=VMEM,
        scratch_shapes=[
            pltpu.VMEM((1, NC), jnp.int32),
            pltpu.VMEM((R, NI), bf16),
            pltpu.VMEM((NC, NI), bf16),
            DMA((3,)),
        ],
    )(idx, res, basis)


def local_body(res_ref, schur_ref, _, out_ref):
    for f in range(FACES):
        out_ref[f] = mm(res_ref[...], schur_ref[:, face_cols(f)]).astype(bf16)


def local_kernel(res, schur, earlier):
    return call(
        local_body,
        jax.ShapeDtypeStruct((FACES, R, FACE), bf16),
        0,
        0,
        vmem=SMALL,
        in_specs=[VMEM, VMEM, ANY],
        out_specs=VMEM,
    )(res, schur, earlier)


def member_onehot(pack_ref):
    digits = pack_ref[:, RZ:, :].astype(f32)
    column = lax.broadcasted_iota(jnp.int32, (C2, NC), 0).astype(f32)
    parts = []
    for c in range(SZ):
        idx = digits[c, 0:1, :] * float(BASE) + digits[c, 1:2, :]
        parts.append((column == idx).astype(bf16))
    return jnp.concatenate(parts, axis=1)


def group_body(pack_ref, restrict_ref, res_ref, top_ref):
    onehot = member_onehot(pack_ref)
    rows = jnp.concatenate([pack_ref[c, :RZ, :] for c in range(SZ)], axis=1)
    group_res = lax.dot_general(rows, onehot, LAST, preferred_element_type=f32)
    res_ref[...] = group_res
    top_ref[...] = mm3(group_res, restrict_ref[...]).astype(bf16)


def group_kernel(pack, restrict):
    return call(
        group_body,
        (jax.ShapeDtypeStruct((RZ, C2), f32), jax.ShapeDtypeStruct((RZ, C2), bf16)),
        0,
        0,
        vmem=8,
        in_specs=[VMEM] * 2,
        out_specs=(VMEM, VMEM),
    )(pack, restrict)


def map_body(top_hbm, restrict_hbm, _, hi_hbm, lo_hbm, top_ref, restrict_ref, hi_ref, lo_ref, sems):
    for c in started([(top_hbm, top_ref), (restrict_hbm, restrict_ref)], sems.at[pl.ds(0, 2)]):
        c.wait()
    t_hi, t_lo = split(top_ref[...])
    r_hi, r_lo = split(restrict_ref[...])
    back = functools.partial(lax.dot_general, dimension_numbers=LAST, preferred_element_type=f32)
    both = back(t_hi, r_hi) + (back(t_hi, r_lo) + back(t_lo, r_hi))
    hi_ref[...], lo_ref[...] = split(both)
    for c in started([(hi_ref, hi_hbm), (lo_ref, lo_hbm)], sems.at[pl.ds(2, 2)]):
        c.wait()


def map_kernel(top_inv, restrict, earlier):
    return call(
        map_body,
        (jax.ShapeDtypeStruct((C2, C2), bf16),) * 2,
        0,
        0,
        vmem=BIG,
        in_specs=[HBM, HBM, ANY],
        out_specs=(HBM, HBM),
        scratch_shapes=[
            pltpu.VMEM((C2, C2), f32),
            pltpu.VMEM((C2, C2), f32),
            pltpu.VMEM((C2, C2), bf16),
            pltpu.VMEM((C2, C2), bf16),
            DMA((4,)),
        ],
    )(top_inv, restrict, earlier)


def own_body(res_ref, group_inv_ref, _, own_ref):
    own_ref[...] = mm3(res_ref[...], group_inv_ref[...])


def own_kernel(group_res, group_inv, later):
    return call(
        own_body,
        jax.ShapeDtypeStruct((RZ, C2), f32),
        0,
        0,
        vmem=SMALL,
        in_specs=[VMEM] * 3,
        out_specs=VMEM,
    )(group_res, group_inv, later)


def solve_body(pack_ref, own_ref, hi_ref, lo_ref, *refs):
    parts, (out_hbm, out_ref, sems) = refs[:-3], refs[-3:]
    onehot = member_onehot(pack_ref)
    top_res = sum(p[...].astype(f32) for p in parts)
    t_hi, t_lo = split(top_res)
    sol = own_ref[...] + mm(t_hi, hi_ref[...]) + (mm(t_hi, lo_ref[...]) + mm(t_lo, hi_ref[...]))
    sol = sol.astype(bf16)
    outs = []
    for i in range(SZ // 2):
        picked = mm(sol, onehot[:, 2 * i * NC : (2 * i + 2) * NC]).astype(bf16)
        out_ref[2 * i], out_ref[2 * i + 1] = picked[:, :NC], picked[:, NC:]
        pair = pl.ds(2 * i, 2)
        outs += started([(out_ref.at[pair], out_hbm.at[pair])], sems.at[pl.ds(i, 1)])
    for c in outs:
        c.wait()


def solve_kernel(pack, own, map_hi, map_lo, parts):
    return call(
        solve_body,
        jax.ShapeDtypeStruct((SZ, RZ, NC), bf16),
        0,
        0,
        vmem=8,
        in_specs=[VMEM] * (4 + len(parts)),
        out_specs=HBM,
        scratch_shapes=[pltpu.VMEM((SZ, RZ, NC), bf16), DMA((SZ // 2,))],
    )(pack, own, map_hi, map_lo, *parts)


def sum_body(count, *refs):
    refs[-1][...] = sum(r[...].astype(f32) for r in refs[:count]).astype(bf16)


def sum_kernel(parts, *earlier):
    return call(
        functools.partial(sum_body, len(parts)),
        jax.ShapeDtypeStruct((RZ, C2), bf16),
        0,
        0,
        vmem=4,
        in_specs=[VMEM] * len(parts) + [ANY] * len(earlier),
        out_specs=VMEM,
    )(*parts, *earlier)


def send_face(meta_ref, slot):
    axis, near = SLOTS[slot]
    if axis != 2:
        axis = axis ^ meta_ref[0, 20]
    odd = meta_ref[0, 18 + axis]
    return 2 * axis + (1 - odd if near else odd)


def update_body(meta_ref, back_ref, basis_ref, local_ref, *refs):
    rows_ref = refs[FACES]
    for c in range(SZ):
        for a in range(SX):
            start = (a * SZ + c) * RX
            rows_ref[start : start + RX, :] = back_ref[c, a * RX : (a + 1) * RX, :]
    rows = rows_ref[...]
    for e, send_ref in enumerate(refs[:FACES]):
        f = send_face(meta_ref, e)
        cols = pl.ds(pl.multiple_of(f * FACE, FACE), FACE)
        update = local_ref[f].astype(f32) + mm(rows, basis_ref[:, cols])
        turned = jnp.concatenate([update[:, BW:], update[:, :BW]], axis=1)
        send_ref[...] = jnp.where(meta_ref[0, 2 * f] == 1, turned, update).astype(bf16)


def update_kernel(meta, back, basis, local):
    return call(
        update_body,
        (jax.ShapeDtypeStruct((R, FACE), bf16),) * FACES,
        0,
        0,
        vmem=SMALL,
        in_specs=[SMEM] + [VMEM] * 3,
        out_specs=(VMEM,) * FACES,
        scratch_shapes=[pltpu.VMEM((R, NC), bf16)],
    )(meta, back, basis, local)


def last_body(slots, meta_ref, *refs):
    count = len(slots)
    out_hbm, out_ref, out_sems = refs[-3:]
    outs = []
    for i, slot in enumerate(slots):
        f = send_face(meta_ref, slot)
        own = refs[i][...]
        both = (own + refs[count + i][...]) * jnp.asarray(0.5, bf16)
        out_ref[i] = jnp.where(meta_ref[0, 12 + f] == 1, both, own)
        pairs = []
        for k in range(2):
            block = 2 * f + meta_ref[0, 2 * f + k]
            pairs.append((out_ref.at[i, :, pl.ds(k * BW, BW)], out_hbm.at[:, block_cols(block)]))
        outs += started(pairs, out_sems.at[pl.ds(2 * i, 2)])
    for c in outs:
        c.wait()


def last_kernel(slots, meta, sends, gots, *partial):
    count = len(slots)
    return call(
        functools.partial(last_body, slots),
        jax.ShapeDtypeStruct((R, NI), bf16),
        0,
        0,
        vmem=SMALL,
        in_specs=[SMEM] + [VMEM] * (2 * count) + [HBM] * len(partial),
        out_specs=HBM,
        input_output_aliases={1 + 2 * count: 0} if partial else {},
        scratch_shapes=[pltpu.VMEM((count, R, FACE), bf16), DMA((2 * count,))],
    )(meta, *[sends[i] for i in slots], *[gots[i] for i in slots], *partial)


def permute(x, target):
    pairs = []
    for a in range(SX):
        for b in range(SY):
            for c in range(SZ):
                ta, tb, tc = target(a, b, c)
                pairs.append(((a * SY + b) * SZ + c, (ta * SY + tb) * SZ + tc))
    return lax.ppermute(x, ("gx", "gy", "gz"), pairs)


def group_of_four(a, b, c, d, turn):
    return (a ^ d, b, c) if c % 2 == turn else (a, b ^ d, c)


def beside(at, count, near):
    return at ^ 1 if near else ((at + 1) ^ 1) - 1 if 0 < at < count - 1 else count - 1 - at


def face_target(a, b, c, slot):
    axis, near = SLOTS[slot]
    if axis == 2:
        return a, b, beside(c, SZ, near)
    if axis == c % 2:
        return beside(a, SX, near), b, c
    return a, beside(b, SY, near), c


def per_device(
    residual,
    schur_inverse,
    coarse_basis,
    coarse_index,
    block_slot,
    group_inverse,
    group_restrict,
    top_inverse,
):
    res = residual[0, 0, 0]
    schur = schur_inverse[0, 0, 0]
    basis = coarse_basis[0, 0, 0]
    idx = coarse_index.reshape(1, NC)
    group_inv = group_inverse[0, 0]
    restrict = group_restrict[0, 0]
    place = [lax.axis_index(axis) for axis in ("gx", "gy", "gz")]
    facts = []
    for at, count in zip(place, (SX, SY, SZ)):
        facts += [at > 0, at < count - 1]
    facts += [at % 2 for at in place]
    facts = jnp.stack([jnp.asarray(v, jnp.int32) for v in facts])
    meta = jnp.concatenate([block_slot.reshape(2 * FACES), facts]).reshape(1, -1)

    pack = coarse_kernel(idx, res, basis)
    top_map = map_kernel(top_inverse, restrict, pack)
    pack = lax.optimization_barrier((lax.all_to_all(pack, "gz", 0, 0), top_map[0]))[0]
    group_res, part = group_kernel(pack, restrict)
    own = own_kernel(group_res, group_inv, res)
    for turn, earlier in ((0, ()), (1, (own,))):
        gots = [part]
        for d in (1, 3, 2):
            gots.append(permute(part, functools.partial(group_of_four, d=d, turn=turn)))
        part = sum_kernel(gots, *earlier)
    parts = [part, permute(part, lambda a, b, c: (a, SY - 1 - b, c))]
    back = solve_kernel(pack, own, *top_map, parts)
    local = local_kernel(res, schur, back)
    back = lax.all_to_all(back, "gz", 0, 0)
    sends = update_kernel(meta, back, basis, local)
    gots = [permute(x, functools.partial(face_target, slot=i)) for i, x in enumerate(sends)]
    out = last_kernel((0, 1), meta, sends, gots)
    out = last_kernel((2, 3, 4, 5), meta, sends, gots, out)
    return out.reshape(1, 1, 1, R, NI)


def solution(mesh):
    return jax.shard_map(
        per_device,
        mesh=mesh,
        in_specs=(
            P("gx", "gy", "gz", None, None),
            P("gx", "gy", "gz", None, None),
            P("gx", "gy", "gz", None, None),
            P("gx", "gy", "gz", None),
            P("gx", "gy", "gz", None),
            P("gx", "gy", None, None),
            P("gx", "gy", None, None),
            P(),
        ),
        out_specs=P("gx", "gy", "gz", None, None),
        check_vma=False,
    )
```

```python
import functools

import jax
import jax.numpy as jnp
from jax import lax
from jax.experimental import pallas as pl
from jax.experimental.pallas import tpu as pltpu
from jax.sharding import PartitionSpec as P

BW = 128
FACE = 256
FACES = 6
NI = 1536
NC = 128
C2 = 512
R = 512
SX, SY, SZ = 4, 8, 8
RX = R // (SX * SZ)
RZ = R // SZ
TAIL = 16
PACK = RZ + TAIL
BASE = 16
COST = 1024
BIG = 58
SMALL = 6
SLOTS = ((0, True), (1, True), (0, False), (1, False), (2, False), (2, True))
CHIPS = SZ // 2

LAST = (((1,), (1,)), ((), ()))
FIRST = (((0,), (0,)), ((), ()))
f32 = jnp.float32
bf16 = jnp.bfloat16


def mm(a, b):
    return jnp.dot(a, b, preferred_element_type=f32)


def split(x):
    hi = x.astype(bf16)
    return hi, (x - hi.astype(f32)).astype(bf16)


def mm3(a, b):
    a_hi, a_lo = split(a)
    b_hi, b_lo = split(b)
    return mm(a_hi, b_hi) + (mm(a_hi, b_lo) + mm(a_lo, b_hi))


def block_cols(block):
    return pl.ds(pl.multiple_of(block * BW, BW), BW)


def call(body, out_shape, flops, size, vmem, **kw):
    return pl.pallas_call(
        body,
        out_shape=out_shape,
        cost_estimate=pl.CostEstimate(flops=COST, bytes_accessed=COST, transcendentals=0),
        compiler_params=pltpu.CompilerParams(vmem_limit_bytes=vmem << 20),
        **kw,
    )


SMEM = pl.BlockSpec(memory_space=pltpu.SMEM)
VMEM = pl.BlockSpec(memory_space=pltpu.VMEM)
ANY = pl.BlockSpec(memory_space=pl.ANY)
HBM = pl.BlockSpec(memory_space=pltpu.HBM)
DMA = pltpu.SemaphoreType.DMA


def started(pairs, sems):
    copies = []
    for i, (src, dst) in enumerate(pairs):
        copies.append(pltpu.make_async_copy(src, dst, sems.at[i]))
        copies[-1].start()
    return copies


def face_cols(f):
    return slice(f * FACE, (f + 1) * FACE)


def coarse_body(idx_hbm, res_hbm, basis_hbm, out_ref, idx_ref, res_ref, basis_ref, sems):
    copies = started([(idx_hbm, idx_ref), (basis_hbm, basis_ref), (res_hbm, res_ref)], sems)
    for c in copies:
        c.wait()
    part = lax.dot_general(res_ref[...], basis_ref[...], LAST, preferred_element_type=f32)
    part = part.astype(bf16).reshape(SX, SZ, RX, NC)
    for a in range(SX):
        out_ref[:, a * RX : (a + 1) * RX, :] = part[a]
    idx = idx_ref[...]
    row = lax.broadcasted_iota(jnp.int32, (TAIL, NC), 0)
    digits = jnp.where(row == 0, idx >> 4, jnp.where(row == 1, idx & (BASE - 1), 0))
    digits = digits.astype(f32).astype(bf16)
    out_ref[:, RZ:, :] = jnp.broadcast_to(digits[None], (SZ, TAIL, NC))


def coarse_kernel(idx, res, basis):
    return call(
        coarse_body,
        jax.ShapeDtypeStruct((SZ, PACK, NC), bf16),
        0,
        0,
        vmem=BIG,
        in_specs=[HBM] * 3,
        out_specs=VMEM,
        scratch_shapes=[
            pltpu.VMEM((1, NC), jnp.int32),
            pltpu.VMEM((R, NI), bf16),
            pltpu.VMEM((NC, NI), bf16),
            DMA((3,)),
        ],
    )(idx, res, basis)


def local_body(res_ref, schur_ref, _, out_ref):
    for f in range(FACES):
        out_ref[f] = mm(res_ref[...], schur_ref[:, face_cols(f)]).astype(bf16)


def local_kernel(res, schur, earlier):
    return call(
        local_body,
        jax.ShapeDtypeStruct((FACES, R, FACE), bf16),
        0,
        0,
        vmem=SMALL,
        in_specs=[VMEM, VMEM, ANY],
        out_specs=VMEM,
    )(res, schur, earlier)


def member_onehot(pack_ref):
    digits = pack_ref[:, RZ:, :].astype(f32)
    column = lax.broadcasted_iota(jnp.int32, (C2, NC), 0).astype(f32)
    parts = []
    for c in range(SZ):
        idx = digits[c, 0:1, :] * float(BASE) + digits[c, 1:2, :]
        parts.append((column == idx).astype(bf16))
    return jnp.concatenate(parts, axis=1)


def group_body(pack_ref, restrict_ref, res_ref, top_ref):
    onehot = member_onehot(pack_ref)
    rows = jnp.concatenate([pack_ref[c, :RZ, :] for c in range(SZ)], axis=1)
    group_res = lax.dot_general(rows, onehot, LAST, preferred_element_type=f32)
    res_ref[...] = group_res
    top_ref[...] = mm3(group_res, restrict_ref[...]).astype(bf16)


def group_kernel(pack, restrict):
    return call(
        group_body,
        (jax.ShapeDtypeStruct((RZ, C2), f32), jax.ShapeDtypeStruct((RZ, C2), bf16)),
        0,
        0,
        vmem=8,
        in_specs=[VMEM] * 2,
        out_specs=(VMEM, VMEM),
    )(pack, restrict)


def map_body(top_hbm, restrict_hbm, _, hi_hbm, lo_hbm, top_ref, restrict_ref, hi_ref, lo_ref, sems):
    for c in started([(top_hbm, top_ref), (restrict_hbm, restrict_ref)], sems.at[pl.ds(0, 2)]):
        c.wait()
    t_hi, t_lo = split(top_ref[...])
    r_hi, r_lo = split(restrict_ref[...])
    back = functools.partial(lax.dot_general, dimension_numbers=LAST, preferred_element_type=f32)
    both = back(t_hi, r_hi) + (back(t_hi, r_lo) + back(t_lo, r_hi))
    hi_ref[...], lo_ref[...] = split(both)
    for c in started([(hi_ref, hi_hbm), (lo_ref, lo_hbm)], sems.at[pl.ds(2, 2)]):
        c.wait()


def map_kernel(top_inv, restrict, earlier):
    return call(
        map_body,
        (jax.ShapeDtypeStruct((C2, C2), bf16),) * 2,
        0,
        0,
        vmem=BIG,
        in_specs=[HBM, HBM, ANY],
        out_specs=(HBM, HBM),
        scratch_shapes=[
            pltpu.VMEM((C2, C2), f32),
            pltpu.VMEM((C2, C2), f32),
            pltpu.VMEM((C2, C2), bf16),
            pltpu.VMEM((C2, C2), bf16),
            DMA((4,)),
        ],
    )(top_inv, restrict, earlier)


def own_body(res_ref, group_inv_ref, _, own_ref):
    own_ref[...] = mm3(res_ref[...], group_inv_ref[...])


def own_kernel(group_res, group_inv, later):
    return call(
        own_body,
        jax.ShapeDtypeStruct((RZ, C2), f32),
        0,
        0,
        vmem=SMALL,
        in_specs=[VMEM] * 3,
        out_specs=VMEM,
    )(group_res, group_inv, later)


def base_body(own_ref, hi_ref, lo_ref, part_ref, out_ref):
    part = part_ref[...]
    out_ref[...] = own_ref[...] + (mm(part, hi_ref[...]) + mm(part, lo_ref[...]))


def base_kernel(own, map_hi, map_lo, part):
    return call(
        base_body,
        jax.ShapeDtypeStruct((RZ, C2), f32),
        0,
        0,
        vmem=SMALL,
        in_specs=[VMEM] * 4,
        out_specs=VMEM,
    )(own, map_hi, map_lo, part)


def solve_body(pack_ref, base_ref, hi_ref, lo_ref, got_ref, out_hbm, out_ref, sems):
    onehot = member_onehot(pack_ref)
    got = got_ref[...]
    sol = (base_ref[...] + (mm(got, hi_ref[...]) + mm(got, lo_ref[...]))).astype(bf16)
    outs = []
    for i in range(SZ // 2):
        picked = mm(sol, onehot[:, 2 * i * NC : (2 * i + 2) * NC]).astype(bf16)
        out_ref[2 * i], out_ref[2 * i + 1] = picked[:, :NC], picked[:, NC:]
        pair = pl.ds(2 * i, 2)
        outs += started([(out_ref.at[pair], out_hbm.at[pair])], sems.at[pl.ds(i, 1)])
    for c in outs:
        c.wait()


def solve_kernel(pack, base, map_hi, map_lo, got):
    return call(
        solve_body,
        jax.ShapeDtypeStruct((SZ, RZ, NC), bf16),
        0,
        0,
        vmem=8,
        in_specs=[VMEM] * 5,
        out_specs=HBM,
        scratch_shapes=[pltpu.VMEM((SZ, RZ, NC), bf16), DMA((SZ // 2,))],
    )(pack, base, map_hi, map_lo, got)


def sum_body(count, *refs):
    refs[-1][...] = sum(r[...].astype(f32) for r in refs[:count]).astype(bf16)


def sum_kernel(parts, *earlier):
    return call(
        functools.partial(sum_body, len(parts)),
        jax.ShapeDtypeStruct((RZ, C2), bf16),
        0,
        0,
        vmem=4,
        in_specs=[VMEM] * len(parts) + [ANY] * len(earlier),
        out_specs=VMEM,
    )(*parts, *earlier)


def send_face(meta_ref, slot):
    axis, near = SLOTS[slot]
    if axis != 2:
        axis = axis ^ meta_ref[0, 20]
    odd = meta_ref[0, 18 + axis]
    return 2 * axis + (1 - odd if near else odd)


def update_body(meta_ref, back_ref, basis_ref, local_ref, *refs):
    rows_ref = refs[FACES]
    for c in range(SZ):
        for a in range(SX):
            start = (a * SZ + c) * RX
            rows_ref[start : start + RX, :] = back_ref[c, a * RX : (a + 1) * RX, :]
    rows = rows_ref[...]
    for e, send_ref in enumerate(refs[:FACES]):
        f = send_face(meta_ref, e)
        cols = pl.ds(pl.multiple_of(f * FACE, FACE), FACE)
        update = (local_ref[f].astype(f32) + mm(rows, basis_ref[:, cols])).astype(bf16)
        low, high = update[:, :BW], update[:, BW:]
        swap = meta_ref[0, 2 * f] == 1
        send_ref[:, :BW] = jnp.where(swap, high, low)
        send_ref[:, BW:] = jnp.where(swap, low, high)


def update_kernel(meta, back, basis, local):
    return call(
        update_body,
        (jax.ShapeDtypeStruct((R, FACE), bf16),) * FACES,
        0,
        0,
        vmem=SMALL,
        in_specs=[SMEM] + [VMEM] * 3,
        out_specs=(VMEM,) * FACES,
        scratch_shapes=[pltpu.VMEM((R, NC), bf16)],
    )(meta, back, basis, local)


def last_body(slots, meta_ref, *refs):
    count = len(slots)
    out_hbm, out_ref, out_sems = refs[-3:]
    outs = []
    for i, slot in enumerate(slots):
        f = send_face(meta_ref, slot)
        own = refs[i][...]
        both = (own + refs[count + i][...]) * jnp.asarray(0.5, bf16)
        out_ref[i] = jnp.where(meta_ref[0, 12 + f] == 1, both, own)
        pairs = []
        for k in range(2):
            block = 2 * f + meta_ref[0, 2 * f + k]
            pairs.append((out_ref.at[i, :, pl.ds(k * BW, BW)], out_hbm.at[:, block_cols(block)]))
        outs += started(pairs, out_sems.at[pl.ds(2 * i, 2)])
    for c in outs:
        c.wait()


def last_kernel(slots, meta, sends, gots, *partial):
    count = len(slots)
    return call(
        functools.partial(last_body, slots),
        jax.ShapeDtypeStruct((R, NI), bf16),
        0,
        0,
        vmem=SMALL,
        in_specs=[SMEM] + [VMEM] * (2 * count) + [HBM] * len(partial),
        out_specs=HBM,
        input_output_aliases={1 + 2 * count: 0} if partial else {},
        scratch_shapes=[pltpu.VMEM((count, R, FACE), bf16), DMA((2 * count,))],
    )(meta, *[sends[i] for i in slots], *[gots[i] for i in slots], *partial)


def permute(x, target):
    pairs = []
    for a in range(SX):
        for b in range(SY):
            for c in range(SZ):
                ta, tb, tc = target(a, b, c)
                pairs.append(((a * SY + b) * SZ + c, (ta * SY + tb) * SZ + tc))
    return lax.ppermute(x, ("gx", "gy", "gz"), pairs)


def group_of_four(a, b, c, d, turn):
    return (a ^ d, b, c) if c % 2 == turn else (a, b ^ d, c)


def beside(at, count, near):
    return at ^ 1 if near else ((at + 1) ^ 1) - 1 if 0 < at < count - 1 else count - 1 - at


def face_target(a, b, c, slot):
    axis, near = SLOTS[slot]
    if axis == 2:
        return a, b, beside(c, SZ, near)
    if axis == c % 2:
        return beside(a, SX, near), b, c
    return a, beside(b, SY, near), c


def per_device(
    residual,
    schur_inverse,
    coarse_basis,
    coarse_index,
    block_slot,
    group_inverse,
    group_restrict,
    top_inverse,
):
    res = residual[0, 0, 0]
    schur = schur_inverse[0, 0, 0]
    basis = coarse_basis[0, 0, 0]
    idx = coarse_index.reshape(1, NC)
    group_inv = group_inverse[0, 0]
    restrict = group_restrict[0, 0]
    place = [lax.axis_index(axis) for axis in ("gx", "gy", "gz")]
    facts = []
    for at, count in zip(place, (SX, SY, SZ)):
        facts += [at > 0, at < count - 1]
    facts += [at % 2 for at in place]
    facts = jnp.stack([jnp.asarray(v, jnp.int32) for v in facts])
    meta = jnp.concatenate([block_slot.reshape(2 * FACES), facts]).reshape(1, -1)

    pack = coarse_kernel(idx, res, basis)
    top_map = map_kernel(top_inverse, restrict, pack)
    pack = lax.optimization_barrier((lax.all_to_all(pack, "gz", 0, 0), top_map[0]))[0]
    group_res, part = group_kernel(pack, restrict)
    own = own_kernel(group_res, group_inv, res)
    for turn, earlier in ((0, ()), (1, (own,))):
        gots = [part]
        for d in (1, 3, 2):
            gots.append(permute(part, functools.partial(group_of_four, d=d, turn=turn)))
        part = sum_kernel(gots, *earlier)
    got = permute(part, lambda a, b, c: (a, SY - 1 - b, c))
    base = base_kernel(own, *top_map, part)
    back = solve_kernel(pack, base, *top_map, got)
    local = local_kernel(res, schur, back)
    back = lax.all_to_all(back, "gz", 0, 0)
    sends = update_kernel(meta, back, basis, local)
    gots = [permute(x, functools.partial(face_target, slot=i)) for i, x in enumerate(sends)]
    out = last_kernel((0, 1), meta, sends, gots)
    out = last_kernel((2, 3, 4, 5), meta, sends, gots, out)
    return out.reshape(1, 1, 1, R, NI)


def solution(mesh):
    return jax.shard_map(
        per_device,
        mesh=mesh,
        in_specs=(
            P("gx", "gy", "gz", None, None),
            P("gx", "gy", "gz", None, None),
            P("gx", "gy", "gz", None, None),
            P("gx", "gy", "gz", None),
            P("gx", "gy", "gz", None),
            P("gx", "gy", None, None),
            P("gx", "gy", None, None),
            P(),
        ),
        out_specs=P("gx", "gy", "gz", None, None),
        check_vma=False,
    )
```

```python
import functools

import jax
import jax.numpy as jnp
from jax import lax
from jax.experimental import pallas as pl
from jax.experimental.pallas import tpu as pltpu
from jax.sharding import PartitionSpec as P

BW = 128
FACE = 256
FACES = 6
NI = 1536
NC = 128
C2 = 512
R = 512
SX, SY, SZ = 4, 8, 8
RX = R // (SX * SZ)
RZ = R // SZ
TAIL = 16
PACK = RZ + TAIL
BASE = 16
COST = 1024
BIG = 58
SMALL = 6
SLOTS = ((0, True), (1, True), (0, False), (1, False), (2, False), (2, True))
CHIPS = SZ // 2

LAST = (((1,), (1,)), ((), ()))
FIRST = (((0,), (0,)), ((), ()))
f32 = jnp.float32
bf16 = jnp.bfloat16


def mm(a, b):
    return jnp.dot(a, b, preferred_element_type=f32)


def split(x):
    hi = x.astype(bf16)
    return hi, (x - hi.astype(f32)).astype(bf16)


def mm3(a, b):
    a_hi, a_lo = split(a)
    b_hi, b_lo = split(b)
    return mm(a_hi, b_hi) + (mm(a_hi, b_lo) + mm(a_lo, b_hi))


def block_cols(block):
    return pl.ds(pl.multiple_of(block * BW, BW), BW)


def call(body, out_shape, flops, size, vmem, **kw):
    return pl.pallas_call(
        body,
        out_shape=out_shape,
        cost_estimate=pl.CostEstimate(flops=COST, bytes_accessed=COST, transcendentals=0),
        compiler_params=pltpu.CompilerParams(vmem_limit_bytes=vmem << 20),
        **kw,
    )


SMEM = pl.BlockSpec(memory_space=pltpu.SMEM)
VMEM = pl.BlockSpec(memory_space=pltpu.VMEM)
ANY = pl.BlockSpec(memory_space=pl.ANY)
HBM = pl.BlockSpec(memory_space=pltpu.HBM)
DMA = pltpu.SemaphoreType.DMA


def started(pairs, sems):
    copies = []
    for i, (src, dst) in enumerate(pairs):
        copies.append(pltpu.make_async_copy(src, dst, sems.at[i]))
        copies[-1].start()
    return copies


def face_cols(f):
    return slice(f * FACE, (f + 1) * FACE)


def coarse_body(idx_hbm, res_hbm, basis_hbm, out_ref, idx_ref, res_ref, basis_ref, sems):
    copies = started([(idx_hbm, idx_ref), (basis_hbm, basis_ref), (res_hbm, res_ref)], sems)
    copies[0].wait()
    idx = idx_ref[...]
    row = lax.broadcasted_iota(jnp.int32, (TAIL, NC), 0)
    digits = jnp.where(row == 0, idx >> 4, jnp.where(row == 1, idx & (BASE - 1), 0))
    digits = digits.astype(f32).astype(bf16)
    out_ref[:, RZ:, :] = jnp.broadcast_to(digits[None], (SZ, TAIL, NC))
    for c in copies[1:]:
        c.wait()
    part = lax.dot_general(res_ref[...], basis_ref[...], LAST, preferred_element_type=f32)
    part = part.astype(bf16).reshape(SX, SZ, RX, NC)
    for a in range(SX):
        out_ref[:, a * RX : (a + 1) * RX, :] = part[a]


def coarse_kernel(idx, res, basis):
    return call(
        coarse_body,
        jax.ShapeDtypeStruct((SZ, PACK, NC), bf16),
        0,
        0,
        vmem=BIG,
        in_specs=[HBM] * 3,
        out_specs=VMEM,
        scratch_shapes=[
            pltpu.VMEM((1, NC), jnp.int32),
            pltpu.VMEM((R, NI), bf16),
            pltpu.VMEM((NC, NI), bf16),
            DMA((3,)),
        ],
    )(idx, res, basis)


def local_body(res_ref, schur_ref, _, out_ref):
    for f in range(FACES):
        out_ref[f] = mm(res_ref[...], schur_ref[:, face_cols(f)]).astype(bf16)


def local_kernel(res, schur, earlier):
    return call(
        local_body,
        jax.ShapeDtypeStruct((FACES, R, FACE), bf16),
        0,
        0,
        vmem=SMALL,
        in_specs=[VMEM, VMEM, ANY],
        out_specs=VMEM,
    )(res, schur, earlier)


def member_onehot(pack_ref):
    digits = pack_ref[:, RZ:, :].astype(f32)
    column = lax.broadcasted_iota(jnp.int32, (C2, NC), 0).astype(f32)
    parts = []
    for c in range(SZ):
        idx = digits[c, 0:1, :] * float(BASE) + digits[c, 1:2, :]
        parts.append((column == idx).astype(bf16))
    return jnp.concatenate(parts, axis=1)


def group_body(pack_ref, restrict_ref, res_ref, top_ref):
    onehot = member_onehot(pack_ref)
    rows = jnp.concatenate([pack_ref[c, :RZ, :] for c in range(SZ)], axis=1)
    group_res = lax.dot_general(rows, onehot, LAST, preferred_element_type=f32)
    res_ref[...] = group_res
    top_ref[...] = mm3(group_res, restrict_ref[...]).astype(bf16)


def group_kernel(pack, restrict):
    return call(
        group_body,
        (jax.ShapeDtypeStruct((RZ, C2), f32), jax.ShapeDtypeStruct((RZ, C2), bf16)),
        0,
        0,
        vmem=8,
        in_specs=[VMEM] * 2,
        out_specs=(VMEM, VMEM),
    )(pack, restrict)


def map_body(top_hbm, restrict_hbm, _, hi_hbm, lo_hbm, top_ref, restrict_ref, hi_ref, lo_ref, sems):
    for c in started([(top_hbm, top_ref), (restrict_hbm, restrict_ref)], sems.at[pl.ds(0, 2)]):
        c.wait()
    t_hi, t_lo = split(top_ref[...])
    r_hi, r_lo = split(restrict_ref[...])
    back = functools.partial(lax.dot_general, dimension_numbers=LAST, preferred_element_type=f32)
    both = back(t_hi, r_hi) + (back(t_hi, r_lo) + back(t_lo, r_hi))
    hi_ref[...], lo_ref[...] = split(both)
    for c in started([(hi_ref, hi_hbm), (lo_ref, lo_hbm)], sems.at[pl.ds(2, 2)]):
        c.wait()


def map_kernel(top_inv, restrict, earlier):
    return call(
        map_body,
        (jax.ShapeDtypeStruct((C2, C2), bf16),) * 2,
        0,
        0,
        vmem=BIG,
        in_specs=[HBM, HBM, ANY],
        out_specs=(HBM, HBM),
        scratch_shapes=[
            pltpu.VMEM((C2, C2), f32),
            pltpu.VMEM((C2, C2), f32),
            pltpu.VMEM((C2, C2), bf16),
            pltpu.VMEM((C2, C2), bf16),
            DMA((4,)),
        ],
    )(top_inv, restrict, earlier)


def own_body(res_ref, group_inv_ref, _, own_ref):
    own_ref[...] = mm3(res_ref[...], group_inv_ref[...])


def own_kernel(group_res, group_inv, later):
    return call(
        own_body,
        jax.ShapeDtypeStruct((RZ, C2), f32),
        0,
        0,
        vmem=SMALL,
        in_specs=[VMEM] * 3,
        out_specs=VMEM,
    )(group_res, group_inv, later)


def base_body(own_ref, hi_ref, lo_ref, part_ref, out_ref):
    part = part_ref[...]
    out_ref[...] = own_ref[...] + (mm(part, hi_ref[...]) + mm(part, lo_ref[...]))


def base_kernel(own, map_hi, map_lo, part):
    return call(
        base_body,
        jax.ShapeDtypeStruct((RZ, C2), f32),
        0,
        0,
        vmem=SMALL,
        in_specs=[VMEM] * 4,
        out_specs=VMEM,
    )(own, map_hi, map_lo, part)


def solve_body(pack_ref, base_ref, hi_ref, lo_ref, got_ref, out_hbm, out_ref, sems):
    onehot = member_onehot(pack_ref)
    got = got_ref[...]
    sol = (base_ref[...] + (mm(got, hi_ref[...]) + mm(got, lo_ref[...]))).astype(bf16)
    outs = []
    for i in range(SZ // 2):
        picked = mm(sol, onehot[:, 2 * i * NC : (2 * i + 2) * NC]).astype(bf16)
        out_ref[2 * i], out_ref[2 * i + 1] = picked[:, :NC], picked[:, NC:]
        pair = pl.ds(2 * i, 2)
        outs += started([(out_ref.at[pair], out_hbm.at[pair])], sems.at[pl.ds(i, 1)])
    for c in outs:
        c.wait()


def solve_kernel(pack, base, map_hi, map_lo, got):
    return call(
        solve_body,
        jax.ShapeDtypeStruct((SZ, RZ, NC), bf16),
        0,
        0,
        vmem=8,
        in_specs=[VMEM] * 5,
        out_specs=HBM,
        scratch_shapes=[pltpu.VMEM((SZ, RZ, NC), bf16), DMA((SZ // 2,))],
    )(pack, base, map_hi, map_lo, got)


def sum_body(count, *refs):
    refs[-1][...] = sum(r[...].astype(f32) for r in refs[:count]).astype(bf16)


def sum_kernel(parts, *earlier):
    return call(
        functools.partial(sum_body, len(parts)),
        jax.ShapeDtypeStruct((RZ, C2), bf16),
        0,
        0,
        vmem=4,
        in_specs=[VMEM] * len(parts) + [ANY] * len(earlier),
        out_specs=VMEM,
    )(*parts, *earlier)


def send_face(meta_ref, slot):
    axis, near = SLOTS[slot]
    if axis != 2:
        axis = axis ^ meta_ref[0, 20]
    odd = meta_ref[0, 18 + axis]
    return 2 * axis + (1 - odd if near else odd)


def update_body(meta_ref, back_ref, basis_ref, local_ref, *refs):
    rows_ref = refs[FACES]
    for c in range(SZ):
        for a in range(SX):
            start = (a * SZ + c) * RX
            rows_ref[start : start + RX, :] = back_ref[c, a * RX : (a + 1) * RX, :]
    rows = rows_ref[...]
    for e, send_ref in enumerate(refs[:FACES]):
        f = send_face(meta_ref, e)
        cols = pl.ds(pl.multiple_of(f * FACE, FACE), FACE)
        update = (local_ref[f].astype(f32) + mm(rows, basis_ref[:, cols])).astype(bf16)
        low, high = update[:, :BW], update[:, BW:]
        swap = meta_ref[0, 2 * f] == 1
        send_ref[:, :BW] = jnp.where(swap, high, low)
        send_ref[:, BW:] = jnp.where(swap, low, high)


def update_kernel(meta, back, basis, local):
    return call(
        update_body,
        (jax.ShapeDtypeStruct((R, FACE), bf16),) * FACES,
        0,
        0,
        vmem=SMALL,
        in_specs=[SMEM] + [VMEM] * 3,
        out_specs=(VMEM,) * FACES,
        scratch_shapes=[pltpu.VMEM((R, NC), bf16)],
    )(meta, back, basis, local)


def last_body(slots, meta_ref, *refs):
    count = len(slots)
    out_hbm, out_ref, out_sems = refs[-3:]
    outs = []
    for i, slot in enumerate(slots):
        f = send_face(meta_ref, slot)
        own = refs[i][...]
        both = (own + refs[count + i][...]) * jnp.asarray(0.5, bf16)
        out_ref[i] = jnp.where(meta_ref[0, 12 + f] == 1, both, own)
        pairs = []
        for k in range(2):
            block = 2 * f + meta_ref[0, 2 * f + k]
            pairs.append((out_ref.at[i, :, pl.ds(k * BW, BW)], out_hbm.at[:, block_cols(block)]))
        outs += started(pairs, out_sems.at[pl.ds(2 * i, 2)])
    for c in outs:
        c.wait()


def last_kernel(slots, meta, sends, gots, *partial):
    count = len(slots)
    return call(
        functools.partial(last_body, slots),
        jax.ShapeDtypeStruct((R, NI), bf16),
        0,
        0,
        vmem=SMALL,
        in_specs=[SMEM] + [VMEM] * (2 * count) + [HBM] * len(partial),
        out_specs=HBM,
        input_output_aliases={1 + 2 * count: 0} if partial else {},
        scratch_shapes=[pltpu.VMEM((count, R, FACE), bf16), DMA((2 * count,))],
    )(meta, *[sends[i] for i in slots], *[gots[i] for i in slots], *partial)


def permute(x, target):
    pairs = []
    for a in range(SX):
        for b in range(SY):
            for c in range(SZ):
                ta, tb, tc = target(a, b, c)
                pairs.append(((a * SY + b) * SZ + c, (ta * SY + tb) * SZ + tc))
    return lax.ppermute(x, ("gx", "gy", "gz"), pairs)


def group_of_four(a, b, c, d, turn):
    return (a ^ d, b, c) if c % 2 == turn else (a, b ^ d, c)


def beside(at, count, near):
    return at ^ 1 if near else ((at + 1) ^ 1) - 1 if 0 < at < count - 1 else count - 1 - at


def face_target(a, b, c, slot):
    axis, near = SLOTS[slot]
    if axis == 2:
        return a, b, beside(c, SZ, near)
    if axis == c % 2:
        return beside(a, SX, near), b, c
    return a, beside(b, SY, near), c


def per_device(
    residual,
    schur_inverse,
    coarse_basis,
    coarse_index,
    block_slot,
    group_inverse,
    group_restrict,
    top_inverse,
):
    res = residual[0, 0, 0]
    schur = schur_inverse[0, 0, 0]
    basis = coarse_basis[0, 0, 0]
    idx = coarse_index.reshape(1, NC)
    group_inv = group_inverse[0, 0]
    restrict = group_restrict[0, 0]
    place = [lax.axis_index(axis) for axis in ("gx", "gy", "gz")]
    facts = []
    for at, count in zip(place, (SX, SY, SZ)):
        facts += [at > 0, at < count - 1]
    facts += [at % 2 for at in place]
    facts = jnp.stack([jnp.asarray(v, jnp.int32) for v in facts])
    meta = jnp.concatenate([block_slot.reshape(2 * FACES), facts]).reshape(1, -1)

    pack = coarse_kernel(idx, res, basis)
    top_map = map_kernel(top_inverse, restrict, pack)
    pack = lax.optimization_barrier((lax.all_to_all(pack, "gz", 0, 0), top_map[0]))[0]
    group_res, part = group_kernel(pack, restrict)
    own = own_kernel(group_res, group_inv, res)
    for turn, earlier in ((0, ()), (1, (own,))):
        gots = [part]
        for d in (1, 3, 2):
            gots.append(permute(part, functools.partial(group_of_four, d=d, turn=turn)))
        part = sum_kernel(gots, *earlier)
    got = permute(part, lambda a, b, c: (a, SY - 1 - b, c))
    base = base_kernel(own, *top_map, part)
    back = solve_kernel(pack, base, *top_map, got)
    local = local_kernel(res, schur, back)
    back = lax.all_to_all(back, "gz", 0, 0)
    sends = update_kernel(meta, back, basis, local)
    gots = [permute(x, functools.partial(face_target, slot=i)) for i, x in enumerate(sends)]
    out = last_kernel((0, 1), meta, sends, gots)
    out = last_kernel((2, 3, 4, 5), meta, sends, gots, out)
    return out.reshape(1, 1, 1, R, NI)


def solution(mesh):
    return jax.shard_map(
        per_device,
        mesh=mesh,
        in_specs=(
            P("gx", "gy", "gz", None, None),
            P("gx", "gy", "gz", None, None),
            P("gx", "gy", "gz", None, None),
            P("gx", "gy", "gz", None),
            P("gx", "gy", "gz", None),
            P("gx", "gy", None, None),
            P("gx", "gy", None, None),
            P(),
        ),
        out_specs=P("gx", "gy", "gz", None, None),
        check_vma=False,
    )
```
